256 devices in a mesh: batch: 32 (over z, y), tensor: 8 (over x, core).
Axes of the slice: x: 4, y: 4, z: 8, core: 2. Of those that a mesh axis runs over, the one named last changes fastest.
Arguments:
- tokens: bfloat16 [16384, 8192], P('batch', 'tensor'), may hold values from -6 to 6
- projection_weight: bfloat16 [8192, 4096], P('tensor'), may hold values from -0.0625 to 0.0625
- adapter_input_maps: bfloat16 [128, 8192, 64], P('batch', 'tensor'), may hold values from -0.0625 to 0.0625
- adapter_output_maps: bfloat16 [128, 64, 4096], P('batch', None, 'tensor'), may hold values from -0.75 to 0.75
- adapter_store_row: int32 [128], replicated, may hold values from 0 to 127, as said below
- adapter_lists_by_batch: int32 [32, 32], P('batch'), may hold values from 0 to 127, as said below
- request_list_position: int32 [16384, 1], P('batch'), may hold values from 0 to 31; in each aligned block of 512 rows (0 to 511, 512 to 1023, ...) at most 64 rows name the same one
Outputs:
- output: bfloat16 [16384, 4096], P('batch', 'tensor')
The draws below stay inside these ranges and needn't reach their ends.
Inputs may be any that keep to these rules, and one draw needn't show every extreme that they name: A permutation: adapter a lives in store row adapter_store_row[a], and store rows o * 4 to (o + 1) * 4 - 1 sit on index o of batch. `adapter_lists_by_batch`: each row lists 32 different adapters; at most 2 of them sit on one index of batch, and in every row some index holds exactly 2. `request_list_position`: among the 512 requests of one batch at most 64 share one list position, and in some batch one position is shared by exactly 64.
All inputs are finite; a program needn't handle non-finite values.
Results may differ from the reference program's by a relative error of at most 0.0047.
Values may be sent and summed in bfloat16 or wider, within the bound.
A program may use at most 128 MiB of HBM per device.

```python
import math
import jax
import jax.numpy as jnp
import numpy as np
from jax import lax

MODEL_WIDTH = 8192
OUTPUT_HALF = 4096
ADAPTER_RANK = 64
CAP = 2
SLOT_MOST = 64
ADP_DEV = 4
B_DEV = 512
G = 32
STORED_ADAPTERS = 128
TOKENS = 16384
N_BATCH = 32


def shared_tables(key):
    key_place, key_lists = jax.random.split(key)
    placement = jax.random.permutation(key_place, STORED_ADAPTERS).astype(jnp.int32)
    inverse = jnp.argsort(placement).astype(jnp.int32)
    token_count = N_BATCH * CAP
    owner_of = (jnp.arange(token_count) // CAP).astype(jnp.int32)
    copy_of = (jnp.arange(token_count) % CAP).astype(jnp.int32)

    def one_batch(batch_key):
        key_one, key_two, key_three, key_four = jax.random.split(batch_key, 4)
        scores = jax.random.permutation(key_one, token_count).astype(jnp.int32)
        heavy = jax.random.randint(key_two, (), 0, N_BATCH).astype(jnp.int32)
        scores = jnp.where(owner_of == heavy, scores - token_count, scores)
        order = jnp.argsort(scores)[:G]
        local_perm = jax.vmap(lambda inner: jax.random.permutation(inner, ADP_DEV))(jax.random.split(key_three, N_BATCH)).astype(jnp.int32)
        owners = owner_of[order]
        local = local_perm[owners, copy_of[order]]
        chosen = inverse[owners * ADP_DEV + local]
        return chosen[jax.random.permutation(key_four, G)]
    lists = jax.vmap(one_batch)(jax.random.split(key_lists, N_BATCH)).astype(jnp.int32)
    return (placement, lists)


def draw_adapter_store_row(key, part):
    tables = shared_tables(key)
    return tables[0]


def draw_adapter_lists_by_batch(key, part):
    tables = shared_tables(key)
    return tables[1]


def levels(rng, shape, cuts, least, largest):
    def one(axis_at, shards_of):
        heights = jax.random.uniform(jax.random.fold_in(jax.random.fold_in(rng, 6), axis_at), (shards_of,), jnp.float32, least / len(cuts), largest / len(cuts))
        return jnp.repeat(jnp.exp(heights), shape[axis_at] // shards_of).reshape((-1,) + (1,) * (len(shape) - axis_at - 1))

    factor_of = one(*cuts[0])
    for cut in cuts[1:]:
        factor_of = factor_of * one(*cut)
    return factor_of


def shared_out(key, own, number, rows, number_of, top, most, slope):
    sequence = jax.random.permutation(key, number_of)
    heavy_load, ordinary = shares(number_of, rows * top, most, slope, True), shares(number_of, rows * top, most, slope, False)
    places = jnp.arange(number_of)

    def named(sizes, offset_by):
        used = int((sizes > 0).sum())
        fixed = max(1, used // 4)
        shifted = fixed + (places - fixed + offset_by * (used - fixed)) % max(1, number_of - fixed)
        return jnp.zeros((number_of,), jnp.int32).at[sequence[jnp.where(places < fixed, places, shifted)]].set(jnp.asarray(sizes, jnp.int32))

    sizes = jnp.where(number % 4 == 0, named(heavy_load, number // 4), named(ordinary, number - number // 4 - 1))
    mixed = jax.random.permutation(jax.random.fold_in(own, 3), number_of)
    donor, taker = mixed[0:number_of // 2 * 2:2], mixed[1:number_of // 2 * 2:2]
    room = jnp.minimum(sizes[donor] - 1, most - sizes[taker]) // 2
    room = jnp.where((donor == sequence[0]) | (taker == sequence[0]) | (sizes[taker] == 0), 0, jnp.maximum(room, 0))
    shifted = jax.random.randint(jax.random.fold_in(own, 4), (number_of // 2,), 0, 1 << 20) % (room + 1)
    sizes = sizes.at[donor].add(-shifted).at[taker].add(shifted)
    items = jnp.searchsorted(jnp.cumsum(sizes), jnp.arange(rows * top), side="right").astype(jnp.int32)
    grid = items.reshape(top, rows).T
    grid = grid[jax.random.permutation(jax.random.fold_in(own, 1), rows)]
    offset_by = jax.random.randint(jax.random.fold_in(own, 2), (rows, 1), 0, top)
    return jnp.take_along_axis(grid, (jnp.arange(top)[None, :] + offset_by) % top, axis=1)


def shares(amount, total, bound, slope, full):
    weights = [(1 << 20) // math.isqrt(grade ** slope) + 1 for grade in range(1, amount + 1)]
    largest = bound if full else min(bound, max(-(-total // amount), total * weights[0] // sum(weights)))
    least = 1 if total - largest >= amount - 1 else 0
    holding, surplus = [largest] + [least] * (amount - 1), total - largest - least * (amount - 1)
    while surplus > 0:
        candidates = [i for i in range(1, amount) if holding[i] < largest] or [i for i in range(1, amount) if holding[i] < bound]
        whole, budget = sum([weights[i] for i in candidates]), surplus
        for i in candidates:
            extra = min(bound - holding[i], max(1, budget * weights[i] // whole), surplus)
            holding[i] = holding[i] + extra
            surplus = surplus - extra
    return np.array(holding)


def scatter_about(key, shape, deviation, bound, cuts=(), kind=jnp.bfloat16):
    factor_of = levels(key, shape, cuts, -0.22, 0.18) if cuts else 1.0
    drawn = jax.random.normal(key, shape, jnp.float32) * deviation * factor_of
    return jnp.minimum(jnp.maximum(drawn, -bound), bound).astype(kind)


def setup_inputs(seed: int = 0) -> dict:
    keys = jax.random.split(jax.random.key(seed), 8)
    tokens = scatter_about(keys[0], (TOKENS, MODEL_WIDTH), 1.0, 6.0, ((0, 32), (1, 8)))
    projection_weight = scatter_about(keys[1], (MODEL_WIDTH, OUTPUT_HALF), MODEL_WIDTH ** -0.5, 0.0625, ((0, 8),))
    adapter_input_maps = scatter_about(keys[2], (STORED_ADAPTERS, MODEL_WIDTH, ADAPTER_RANK), MODEL_WIDTH ** -0.5, 0.0625, ((0, 32), (1, 8)))
    adapter_output_maps = scatter_about(keys[3], (STORED_ADAPTERS, ADAPTER_RANK, OUTPUT_HALF), ADAPTER_RANK ** -0.5, 0.75, ((0, 32), (2, 8)))
    adapter_store_row = draw_adapter_store_row(jax.random.fold_in(keys[7], 71), 0)
    adapter_lists_by_batch = draw_adapter_lists_by_batch(jax.random.fold_in(keys[7], 71), 0)
    request_list_position_keys = jax.random.split(jax.random.fold_in(keys[6], 1), TOKENS // B_DEV)
    request_list_position_turns = jax.random.permutation(jax.random.fold_in(keys[6], 3), TOKENS // B_DEV)
    request_list_position = jax.vmap(lambda own, number: shared_out(jax.random.fold_in(keys[6], 2), own, number, B_DEV, G, 1, SLOT_MOST, 2))(request_list_position_keys, request_list_position_turns).reshape((TOKENS, 1))
    return dict(tokens=tokens, projection_weight=projection_weight, adapter_input_maps=adapter_input_maps, adapter_output_maps=adapter_output_maps, adapter_store_row=adapter_store_row, adapter_lists_by_batch=adapter_lists_by_batch, request_list_position=request_list_position)


def reference(tokens, projection_weight, adapter_input_maps, adapter_output_maps, adapter_store_row, adapter_lists_by_batch, request_list_position):
    base = jnp.dot(tokens, projection_weight, preferred_element_type=jnp.float32)
    batch_of = (jnp.arange(TOKENS) // B_DEV).astype(jnp.int32)
    adapter = adapter_lists_by_batch[batch_of, request_list_position[:, 0]]
    store_row = adapter_store_row[adapter].astype(jnp.int32)
    rows_blocks = store_row.reshape(TOKENS // 32, 32)
    token_blocks = tokens.reshape(TOKENS // 32, 32, MODEL_WIDTH)

    def one_block(pair):
        block_of_rows, token_block = pair
        input_maps_held = adapter_input_maps[block_of_rows].astype(jnp.float32)
        low_rank = jnp.einsum('td,tdr->tr', token_block.astype(jnp.float32), input_maps_held, precision=lax.Precision.HIGHEST).astype(jnp.bfloat16)
        output_maps_held = adapter_output_maps[block_of_rows].astype(jnp.float32)
        return jnp.einsum('tr,tro->to', low_rank.astype(jnp.float32), output_maps_held, precision=lax.Precision.HIGHEST)

    adapted = lax.map(one_block, (rows_blocks, token_blocks)).reshape(TOKENS, OUTPUT_HALF)
    return (base + 2.0 * adapted).astype(jnp.bfloat16)
```

```python
import jax
import jax.numpy as jnp
from jax import lax
from jax.experimental import pallas as pl
from jax.experimental.pallas import tpu as pltpu
from jax.sharding import PartitionSpec as P

MESH = pl.DeviceIdType.MESH
BF = jnp.bfloat16
F32 = jnp.float32
NT = (((1,), (1,)), ((), ()))
PLUS, MINUS = 0, 1
STREAM_A, STREAM_B0, STREAM_B1 = 0, 1, 2


def kernel(
    tok_h, w_h, a_h, b_h, store_ref, list_ref, pos_ref, out_ref,
    tok_all, a_all, b_all, s_all, s_bc, wbuf, acc,
    mate_send, mate_recv, q, base_own, x_half, x_recv,
    packed, part_recv, low_all, spread, y_send, y_half, y_recv, own_adapted,
    local_sem, w_sem, z_send, z_recv, yt_send, yt_recv, s_send, s_recv,
    m_send, m_recv, x_send_sem, x_recv_sem, p_send, p_recv, g_send, g_recv,
    r_send, r_recv,
):
    b = lax.axis_index("batch")
    t = lax.axis_index("tensor")
    z, y = lax.div(b, 4), lax.rem(b, 4)
    x, c = lax.div(t, 2), lax.rem(t, 2)

    def at_z(d):
        return lax.rem(z + d + 8, 8)

    z_dev = ((at_z(1) * 4 + y, t), (at_z(-1) * 4 + y, t))
    y_dev = ((z * 4 + lax.rem(y + 1, 4), t), (z * 4 + lax.rem(y + 3, 4), t))
    y_far = (z * 4 + lax.rem(y + 2, 4), t)
    x_dev = ((b, lax.rem(x + 1, 4) * 2 + c), (b, lax.rem(x + 3, 4) * 2 + c))
    mate = (b, x * 2 + 1 - c)
    others = [(b, lax.rem(t + k, 8)) for k in range(1, 8)]

    started = []

    def go(copy):
        copy.start()
        started.append(copy)

    def remote(src, dst, send, recv, device):
        return pltpu.make_async_remote_copy(
            src_ref=src, dst_ref=dst, send_sem=send, recv_sem=recv,
            device_id=device, device_id_type=MESH,
        )

    tok_local = [
        pltpu.make_async_copy(tok_h.at[pl.ds(256 * i, 256)], tok_all.at[i], local_sem.at[i])
        for i in range(2)
    ]
    a_local = pltpu.make_async_copy(a_h, a_all.at[0], local_sem.at[2])
    b_local = [
        pltpu.make_async_copy(
            b_h.at[:, pl.ds(256 * n, 256)], b_all.at[n, pl.ds(0, 256)], local_sem.at[3 + n]
        )
        for n in range(2)
    ]
    chips = [lax.rem(x + d, 4) for d in (2, 1, 3, 0)]
    w_local = []
    for j in range(8):
        column = (chips[j % 4] * 2 + (1 - c if j < 4 else c)) * 512
        w_local.append(
            pltpu.make_async_copy(
                w_h.at[:, pl.ds(pl.multiple_of(column, 512), 512)], wbuf.at[j], w_sem.at[j]
            )
        )
    for copy in tok_local + w_local[:2] + [a_local] + w_local[2:] + b_local:
        copy.start()

    barrier = pltpu.get_barrier_semaphore()
    partners = [z_dev[0], z_dev[1], y_dev[0], y_dev[1], y_far] + others
    for device in partners:
        pl.semaphore_signal(barrier, inc=1, device_id=device, device_id_type=MESH)

    list_row = jnp.broadcast_to(list_ref[...].astype(F32), (32, 32))
    eye = lax.broadcasted_iota(jnp.int32, (32, 32), 0) == lax.broadcasted_iota(jnp.int32, (32, 32), 1)
    list_col = jnp.sum(jnp.where(eye, list_row, 0.0), axis=1, keepdims=True)
    lane_a = lax.broadcasted_iota(jnp.int32, (32, 128), 1).astype(F32)
    rows_col = jnp.sum(
        jnp.where(lane_a == list_col, jnp.broadcast_to(store_ref[...].astype(F32), (32, 128)), 0.0),
        axis=1, keepdims=True,
    )
    hot = lax.broadcasted_iota(jnp.int32, (32, 512), 0) == jnp.broadcast_to(pos_ref[...], (32, 512))
    s_row = jnp.sum(jnp.where(hot, jnp.broadcast_to(rows_col, (32, 512)), 0.0), axis=0, keepdims=True)
    s_all[0] = jnp.broadcast_to(s_row, (8, 512))

    pl.semaphore_wait(barrier, len(partners))

    s_copies = [
        remote(s_all.at[0], s_all.at[slot], s_send.at[slot - 1], s_recv.at[slot - 1], device)
        for slot, device in ((1, y_dev[0]), (2, y_dev[1]), (3, y_far))
    ]

    def z_place(stream, slot, half):
        if stream == STREAM_A:
            return a_all.at[slot, pl.ds(half * 128, 128)]
        return b_all.at[stream - 1, pl.ds(slot * 256 + half * 128, 128)]

    def z_own(stream, half):
        if stream == STREAM_A:
            return a_h.at[pl.ds(half * 128, 128)]
        return b_h.at[pl.ds(half * 128, 128), pl.ds(256 * (stream - 1), 256)]

    def z_slot(way, d):
        return 7 if d == 4 else d + 3 * way

    def z_copy(stream, way, k):
        d, half = k // 2 + 1, (k % 2) ^ way
        src = z_own(stream, half) if d == 1 else z_place(stream, z_slot(way, d - 1), half)
        i = stream * 14 + way * 7 + k
        return remote(src, z_place(stream, z_slot(way, d), half), z_send.at[i], z_recv.at[i], z_dev[way])

    z_all = [[[z_copy(s, w, k) for k in range(7)] for w in range(2)] for s in range(3)]

    def z_begin(stream):
        for k in range(2):
            for way in range(2):
                go(z_all[stream][way][k])

    def z_serve(stream, k):
        for way in range(2):
            z_all[stream][way][k].wait_recv()
            if k < 5:
                go(z_all[stream][way][k + 2])

    def y_copy(way, k):
        half = (k % 2) ^ way
        if k < 2:
            src, dst = tok_h.at[pl.ds(256 * half, 256)], tok_all.at[2 * (1 + way) + half]
        else:
            src, dst = tok_all.at[2 * (1 + way) + half], tok_all.at[6 + half]
        return remote(src, dst, yt_send.at[way * 3 + k], yt_recv.at[way * 3 + k], y_dev[way])

    y_tok = [[y_copy(w, k) for k in range(3)] for w in range(2)]

    for copy in s_copies:
        go(copy)
    z_begin(STREAM_A)
    for k in range(2):
        for way in range(2):
            go(y_tok[way][k])

    for copy in tok_local:
        copy.wait()

    mate_copies = [
        remote(mate_send.at[j], mate_recv.at[j], m_send.at[j], m_recv.at[j], mate) for j in range(4)
    ]

    def base_tile(i, j):
        return jnp.dot(tok_all[i], wbuf[j], preferred_element_type=F32)

    for j in range(4):
        w_local[j].wait()

        @pl.loop(0, 2)
        def _(i):
            mate_send[j, i] = base_tile(i, j).astype(BF)

        go(mate_copies[j])

    def base_mine(j):
        w_local[4 + j].wait()
        mate_copies[j].wait_recv()

        @pl.loop(0, 2)
        def _(i):
            total = base_tile(i, 4 + j) + mate_recv[j, i].astype(F32)
            if j < 3:
                q[j, i] = total.astype(BF)
            else:
                base_own[i] = total

    def x_copy(n, src, dst, way):
        return remote(src, dst, x_send_sem.at[n], x_recv_sem.at[n], x_dev[way])

    x_first = [x_copy(w, q.at[0, w], x_half.at[w], w) for w in range(2)]
    x_plain = [x_copy(2 + w, q.at[1 + w, 1 - w], x_recv.at[w, 1 - w], w) for w in range(2)]
    x_added = [x_copy(4 + w, q.at[1 + w, w], x_recv.at[w, w], w) for w in range(2)]

    base_mine(0)
    for copy in x_first:
        go(copy)
    base_mine(1)
    go(x_plain[0])
    base_mine(2)
    go(x_plain[1])
    z_serve(STREAM_A, 0)
    base_mine(3)

    for copy in s_copies:
        copy.wait_recv()
    for slot in range(4):
        for block in range(4):
            row = s_all[slot, 0:1, 128 * block:128 * (block + 1)]
            tile = jnp.broadcast_to(row, (128, 128)).T
            s_bc[2 * slot + block // 2, 128 * (block % 2):128 * (block % 2 + 1)] = tile

    z_serve(STREAM_A, 1)
    for way in range(2):
        y_tok[way][0].wait_recv()
        go(y_tok[way][2])
    for way in range(2):
        x_first[way].wait_recv()
        q[1 + way, way] = (q[1 + way, way].astype(F32) + x_half[way].astype(F32)).astype(BF)
        go(x_added[way])

    quarter = lax.broadcasted_iota(jnp.int32, (256, 128), 1) // 64

    def first_row(slot):
        d = 4 if slot == 7 else (-slot if slot < 4 else slot - 3)
        return at_z(d) * 16 + y * 4

    def low(slot, lowest, highest):
        rows = [(first_row(slot) + 2 * h + quarter).astype(F32) for h in range(2)]

        @pl.loop(lowest, highest)
        def _(i):
            product = lax.dot_general(tok_all[i], a_all[slot], NT, preferred_element_type=F32)
            for h in range(2):
                kept = jnp.where(s_bc[i] == rows[h], product[:, 128 * h:128 * (h + 1)], 0.0)
                if slot == 0:
                    acc[i, :, 128 * h:128 * (h + 1)] = kept
                else:
                    acc[i, :, 128 * h:128 * (h + 1)] += kept

    a_local.wait()
    for slot in (0, 1, 4):
        low(slot, 0, 2)
    z_serve(STREAM_A, 2)
    z_serve(STREAM_A, 3)
    for way in range(2):
        y_tok[way][1].wait_recv()
    for slot in (0, 1, 4):
        low(slot, 2, 6)
    for slot in (2, 5):
        low(slot, 0, 6)
    z_serve(STREAM_A, 4)
    z_serve(STREAM_A, 5)
    z_begin(STREAM_B0)
    for way in range(2):
        y_tok[way][2].wait_recv()
    for slot in (0, 1, 4, 2, 5):
        low(slot, 6, 8)
    for slot in (3, 6):
        low(slot, 0, 8)
    z_serve(STREAM_A, 6)
    z_begin(STREAM_B1)
    low(7, 0, 8)

    lane = lax.broadcasted_iota(jnp.int32, (256, 128), 1)

    def folded(i):
        h = acc[i, :, 0:128] + acc[i, :, 128:256]
        return h + pltpu.roll(h, 64, 1)

    @pl.loop(0, 4)
    def _(i):
        both = jnp.where(lane < 64, folded(i), folded(i + 4))
        packed[2 * i] = both[0:128]
        packed[2 * i + 1] = both[128:256]

    p_copies = [
        remote(packed.at[lax.rem(t + k, 8)], part_recv.at[k - 1], p_send.at[k - 1], p_recv.at[k - 1], others[k - 1])
        for k in range(1, 8)
    ]
    for copy in p_copies:
        go(copy)
    for k in range(3):
        z_serve(STREAM_B0, k)
    for copy in p_copies:
        copy.wait_recv()
    total = packed[t]
    for k in range(7):
        total += part_recv[k]
    low_all[t] = total.astype(BF)
    g_copies = [
        remote(low_all.at[t], low_all.at[t], g_send.at[k - 1], g_recv.at[k - 1], others[k - 1])
        for k in range(1, 8)
    ]
    for copy in g_copies:
        go(copy)
    for k in range(3, 5):
        z_serve(STREAM_B0, k)
    z_serve(STREAM_B1, 0)
    z_serve(STREAM_B1, 1)
    for k in range(1, 8):
        remote(
            low_all.at[t], low_all.at[lax.rem(t + 8 - k, 8)], g_send.at[k - 1], g_recv.at[k - 1], others[k - 1]
        ).wait_recv()

    @pl.loop(0, 8)
    def _(i):
        r = lax.rem(i, 4)
        v = jnp.concatenate([low_all[2 * r], low_all[2 * r + 1]], axis=0).astype(F32)
        turned = pltpu.roll(v, 64, 1)
        both = jnp.where((lane < 64) == (i < 4), v, turned)
        rows = s_bc[i]
        for slot in range(8):
            for h in range(2):
                want = (first_row(slot) + 2 * h + quarter).astype(F32)
                column = slot * 256 + 128 * h
                spread[i, :, column:column + 128] = jnp.where(rows == want, both, 0.0).astype(BF)

    for copy in b_local:
        copy.wait()

    def r_copy(n, half, index, src, dst, way):
        i = n * 6 + index
        return remote(src, dst, r_send.at[i], r_recv.at[i], y_dev[way])

    r_first = [[r_copy(n, w, w, y_send.at[n, 4 + w], y_half.at[n, w], w) for w in range(2)] for n in range(2)]
    r_plain = [
        [r_copy(n, 1 - w, 2 + w, y_send.at[n, 2 * (1 - w) + 1 - w], y_recv.at[n, w, 1 - w], w) for w in range(2)]
        for n in range(2)
    ]
    r_added = [
        [r_copy(n, w, 4 + w, y_send.at[n, 2 * (1 - w) + w], y_recv.at[n, w, w], w) for w in range(2)]
        for n in range(2)
    ]

    def adapted(n, i):
        return jnp.dot(spread[i], b_all[n], preferred_element_type=F32)

    def send_back(n):
        @pl.loop(6, 8)
        def _(i):
            y_send[n, i - 2] = adapted(n, i).astype(BF)

        for way in range(2):
            go(r_first[n][way])

        @pl.loop(2, 6)
        def _(i):
            y_send[n, i - 2] = adapted(n, i).astype(BF)

        for way in range(2):
            go(r_plain[n][way])

    def send_added(n):
        for way in range(2):
            r_first[n][way].wait_recv()
            place = 2 * (1 - way) + way
            y_send[n, place] = (y_send[n, place].astype(F32) + y_half[n, way].astype(F32)).astype(BF)
            go(r_added[n][way])

    def mine(n):
        @pl.loop(0, 2)
        def _(i):
            own_adapted[n, i] = adapted(n, i)

    def finish(n):
        for way in range(2):
            r_plain[n][way].wait_recv()
            r_added[n][way].wait_recv()
        for i in range(2):
            columns = pl.ds(256 * n, 256)
            base = base_own[i, :, columns] + (
                x_recv[0, i, :, columns].astype(F32) + x_recv[1, i, :, columns].astype(F32)
            )
            extra = own_adapted[n, i] + (y_recv[n, 0, i].astype(F32) + y_recv[n, 1, i].astype(F32))
            out_ref[pl.ds(256 * i, 256), columns] = (base + 2.0 * extra).astype(BF)

    z_serve(STREAM_B0, 5)
    z_serve(STREAM_B0, 6)
    z_serve(STREAM_B1, 2)
    send_back(0)
    z_serve(STREAM_B1, 3)
    z_serve(STREAM_B1, 4)
    send_added(0)
    mine(0)
    z_serve(STREAM_B1, 5)
    z_serve(STREAM_B1, 6)
    send_back(1)
    mine(1)
    send_added(1)
    for way in range(2):
        x_plain[way].wait_recv()
        x_added[way].wait_recv()
    finish(0)
    finish(1)
    for copy in started:
        copy.wait_send()


def body(
    tokens,
    projection_weight,
    adapter_input_maps,
    adapter_output_maps,
    adapter_store_row,
    adapter_lists_by_batch,
    request_list_position,
):
    dma = pltpu.SemaphoreType.DMA
    vmem = pltpu.VMEM
    hbm = pl.BlockSpec(memory_space=pl.ANY)
    near = pl.BlockSpec(memory_space=pltpu.VMEM)
    return pl.pallas_call(
        kernel,
        out_shape=jax.ShapeDtypeStruct((512, 512), BF),
        in_specs=[hbm] * 4 + [near] * 3,
        out_specs=near,
        scratch_shapes=[
            vmem((8, 256, 1024), BF),
            vmem((8, 256, 1024), BF),
            vmem((2, 2048, 256), BF),
            vmem((4, 8, 512), F32),
            vmem((8, 256, 128), F32),
            vmem((8, 1024, 512), BF),
            vmem((8, 256, 256), F32),
            vmem((4, 2, 256, 512), BF),
            vmem((4, 2, 256, 512), BF),
            vmem((3, 2, 256, 512), BF),
            vmem((2, 256, 512), F32),
            vmem((2, 256, 512), BF),
            vmem((2, 2, 256, 512), BF),
            vmem((8, 128, 128), F32),
            vmem((7, 128, 128), F32),
            vmem((8, 128, 128), BF),
            vmem((8, 256, 2048), BF),
            vmem((2, 6, 256, 256), BF),
            vmem((2, 2, 256, 256), BF),
            vmem((2, 2, 2, 256, 256), BF),
            vmem((2, 2, 256, 256), F32),
            dma((5,)), dma((8,)), dma((42,)), dma((42,)), dma((6,)), dma((6,)), dma((3,)), dma((3,)),
            dma((4,)), dma((4,)), dma((6,)), dma((6,)), dma((7,)), dma((7,)), dma((7,)), dma((7,)),
            dma((12,)), dma((12,)),
        ],
        compiler_params=pltpu.CompilerParams(
            collective_id=0, has_side_effects=True, vmem_limit_bytes=56 * 1024 * 1024
        ),
        cost_estimate=pl.CostEstimate(flops=17_200_000_000, bytes_accessed=13_000_000, transcendentals=0),
    )(
        tokens,
        projection_weight,
        jnp.swapaxes(adapter_input_maps, 1, 2).reshape(256, 1024),
        adapter_output_maps.reshape(256, 512),
        adapter_store_row.reshape(1, 128),
        adapter_lists_by_batch,
        request_list_position.reshape(1, 512),
    )


def solution(mesh):
    in_specs = (
        P("batch", "tensor"),
        P("tensor", None),
        P("batch", "tensor", None),
        P("batch", None, "tensor"),
        P(),
        P("batch", None),
        P("batch", None),
    )
    out_specs = P("batch", "tensor")
    return jax.shard_map(body, mesh=mesh, in_specs=in_specs, out_specs=out_specs, check_vma=False)
```

```python
import jax
import jax.numpy as jnp
from jax import lax
from jax.experimental import pallas as pl
from jax.experimental.pallas import tpu as pltpu
from jax.sharding import PartitionSpec as P

MESH = pl.DeviceIdType.MESH
BF = jnp.bfloat16
F32 = jnp.float32
NT = (((1,), (1,)), ((), ()))
PLUS, MINUS = 0, 1
STREAM_A = 0
CUTS = ((0, 256), (256, 256))


def kernel(
    tok_h, w_h, a_h, b_h, store_ref, list_ref, pos_ref, out_ref,
    tok_all, a_all, b_all_0, b_all_1, s_all, s_bc, wbuf, acc,
    mate_send, mate_recv, q, base_own, x_half, x_recv,
    packed_0, packed_1, part_0, part_1, low_0, low_1, spread,
    y_send_0, y_half_0, y_recv_0, own_0, y_send_1, y_half_1, y_recv_1, own_1,
    local_sem, w_sem, z_send, z_recv, yt_send, yt_recv, s_send, s_recv,
    m_send, m_recv, x_send_sem, x_recv_sem, p_send, p_recv, g_send, g_recv,
    r_send, r_recv,
):
    b_all = (b_all_0, b_all_1)
    packed, part_recv, low_all = (packed_0, packed_1), (part_0, part_1), (low_0, low_1)
    y_send, y_half = (y_send_0, y_send_1), (y_half_0, y_half_1)
    y_recv, own_adapted = (y_recv_0, y_recv_1), (own_0, own_1)
    b = lax.axis_index("batch")
    t = lax.axis_index("tensor")
    z, y = lax.div(b, 4), lax.rem(b, 4)
    x, c = lax.div(t, 2), lax.rem(t, 2)

    def at_z(d):
        return lax.rem(z + d + 8, 8)

    z_dev = ((at_z(1) * 4 + y, t), (at_z(-1) * 4 + y, t))
    y_dev = ((z * 4 + lax.rem(y + 1, 4), t), (z * 4 + lax.rem(y + 3, 4), t))
    y_far = (z * 4 + lax.rem(y + 2, 4), t)
    x_dev = ((b, lax.rem(x + 1, 4) * 2 + c), (b, lax.rem(x + 3, 4) * 2 + c))
    mate = (b, x * 2 + 1 - c)
    others = [(b, lax.rem(t + k, 8)) for k in range(1, 8)]

    started = []

    def go(copy):
        copy.start()
        started.append(copy)

    def remote(src, dst, send, recv, device):
        return pltpu.make_async_remote_copy(
            src_ref=src, dst_ref=dst, send_sem=send, recv_sem=recv,
            device_id=device, device_id_type=MESH,
        )

    tok_local = [pltpu.make_async_copy(tok_h, tok_all.at[0], local_sem.at[0])]
    a_local = pltpu.make_async_copy(a_h, a_all.at[0], local_sem.at[2])
    b_local = [
        pltpu.make_async_copy(
            b_h.at[:, pl.ds(*CUTS[n])], b_all[n].at[pl.ds(0, 256)], local_sem.at[3 + n]
        )
        for n in range(2)
    ]
    chips = [lax.rem(x + d, 4) for d in (2, 1, 3, 0)]
    w_local = []
    for j in range(8):
        column = (chips[j % 4] * 2 + (1 - c if j < 4 else c)) * 512
        w_local.append(
            pltpu.make_async_copy(
                w_h.at[:, pl.ds(pl.multiple_of(column, 512), 512)], wbuf.at[j], w_sem.at[j]
            )
        )
    for copy in tok_local + w_local[:2] + [a_local] + w_local[2:] + b_local:
        copy.start()

    barrier = pltpu.get_barrier_semaphore()
    partners = [z_dev[0], z_dev[1], y_dev[0], y_dev[1], y_far] + others
    for device in partners:
        pl.semaphore_signal(barrier, inc=1, device_id=device, device_id_type=MESH)

    list_row = jnp.broadcast_to(list_ref[...].astype(F32), (32, 32))
    eye = lax.broadcasted_iota(jnp.int32, (32, 32), 0) == lax.broadcasted_iota(jnp.int32, (32, 32), 1)
    list_col = jnp.sum(jnp.where(eye, list_row, 0.0), axis=1, keepdims=True)
    lane_a = lax.broadcasted_iota(jnp.int32, (32, 128), 1).astype(F32)
    rows_col = jnp.sum(
        jnp.where(lane_a == list_col, jnp.broadcast_to(store_ref[...].astype(F32), (32, 128)), 0.0),
        axis=1, keepdims=True,
    )
    hot = lax.broadcasted_iota(jnp.int32, (32, 512), 0) == jnp.broadcast_to(pos_ref[...], (32, 512))
    s_row = jnp.sum(jnp.where(hot, jnp.broadcast_to(rows_col, (32, 512)), 0.0), axis=0, keepdims=True)
    s_all[0] = jnp.broadcast_to(s_row, (8, 512))

    pl.semaphore_wait(barrier, len(partners))

    s_copies = [
        remote(s_all.at[0], s_all.at[slot], s_send.at[slot - 1], s_recv.at[slot - 1], device)
        for slot, device in ((1, y_dev[0]), (2, y_dev[1]), (3, y_far))
    ]

    def z_rows(way, k):
        return k // 2 + 1, ((k % 2) ^ way) * 128, 128

    def z_place(stream, slot, row, rows):
        if stream == STREAM_A:
            return a_all.at[slot, pl.ds(row, rows)]
        return b_all[stream - 1].at[pl.ds(slot * 256 + row, rows)]

    def z_own(stream, row, rows):
        if stream == STREAM_A:
            return a_h.at[pl.ds(row, rows)]
        return b_h.at[pl.ds(row, rows), pl.ds(*CUTS[stream - 1])]

    def z_slot(way, d):
        return 7 if d == 4 else d + 3 * way

    def z_copy(stream, way, k):
        d, row, rows = z_rows(way, k)
        src = z_own(stream, row, rows) if d == 1 else z_place(stream, z_slot(way, d - 1), row, rows)
        i = stream * 14 + way * 7 + k
        return remote(
            src, z_place(stream, z_slot(way, d), row, rows), z_send.at[i], z_recv.at[i], z_dev[way]
        )

    z_all = [[[z_copy(s, w, k) for k in range(7)] for w in range(2)] for s in range(3)]

    def z_begin(stream, *steps):
        for k in steps:
            for way in range(2):
                go(z_all[stream][way][k])

    def z_serve(stream, k):
        for way in range(2):
            z_all[stream][way][k].wait_recv()
            if k < 5:
                go(z_all[stream][way][k + 2])

    def y_copy(way, k):
        rows = pl.ds(256 * ((k % 2) ^ way), 256)
        if k < 2:
            src, dst = tok_h.at[rows], tok_all.at[1 + way, rows]
        else:
            src, dst = tok_all.at[1 + way, rows], tok_all.at[3, rows]
        return remote(src, dst, yt_send.at[way * 3 + k], yt_recv.at[way * 3 + k], y_dev[way])

    y_tok = [[y_copy(w, k) for k in range(3)] for w in range(2)]

    for copy in s_copies:
        go(copy)
    z_begin(STREAM_A, 0, 1)
    for k in range(2):
        for way in range(2):
            go(y_tok[way][k])

    for copy in tok_local:
        copy.wait()

    mate_copies = [
        remote(mate_send.at[j], mate_recv.at[j], m_send.at[j], m_recv.at[j], mate) for j in range(4)
    ]

    def base_part(j):
        return jnp.dot(tok_all[0], wbuf[j], preferred_element_type=F32)

    for j in range(4):
        w_local[j].wait()

        part = base_part(j).astype(BF)
        mate_send[j, 0] = part[0:256]
        mate_send[j, 1] = part[256:512]

        go(mate_copies[j])

    def base_mine(j):
        w_local[4 + j].wait()
        mate_copies[j].wait_recv()

        part = base_part(4 + j)
        for i in range(2):
            total = part[256 * i:256 * (i + 1)] + mate_recv[j, i].astype(F32)
            if j < 3:
                q[j, i] = total.astype(BF)
            else:
                base_own[i] = total

    def x_copy(n, src, dst, way):
        return remote(src, dst, x_send_sem.at[n], x_recv_sem.at[n], x_dev[way])

    x_first = [x_copy(w, q.at[0, w], x_half.at[w], w) for w in range(2)]
    x_plain = [x_copy(2 + w, q.at[1 + w, 1 - w], x_recv.at[w, 1 - w], w) for w in range(2)]
    x_added = [x_copy(4 + w, q.at[1 + w, w], x_recv.at[w, w], w) for w in range(2)]

    base_mine(0)
    for copy in x_first:
        go(copy)
    base_mine(1)
    go(x_plain[0])
    base_mine(2)
    go(x_plain[1])
    z_serve(STREAM_A, 0)
    base_mine(3)

    for copy in s_copies:
        copy.wait_recv()
    for slot in range(4):
        for block in range(4):
            row = s_all[slot, 0:1, 128 * block:128 * (block + 1)]
            tile = jnp.broadcast_to(row, (128, 128)).T
            s_bc[slot, 128 * block:128 * (block + 1)] = tile

    z_serve(STREAM_A, 1)
    for way in range(2):
        y_tok[way][0].wait_recv()
        go(y_tok[way][2])
    for way in range(2):
        x_first[way].wait_recv()
        q[1 + way, way] = (q[1 + way, way].astype(F32) + x_half[way].astype(F32)).astype(BF)
        go(x_added[way])

    quarter = lax.broadcasted_iota(jnp.int32, (512, 128), 1) // 64

    def first_row(slot):
        d = 4 if slot == 7 else (-slot if slot < 4 else slot - 3)
        return at_z(d) * 16 + y * 4

    def low(slot, lowest, highest):
        rows = [(first_row(slot) + 2 * h + quarter).astype(F32) for h in range(2)]

        @pl.loop(lowest, highest)
        def _(i):
            product = lax.dot_general(tok_all[i], a_all[slot], NT, preferred_element_type=F32)
            for h in range(2):
                kept = jnp.where(s_bc[i] == rows[h], product[:, 128 * h:128 * (h + 1)], 0.0)
                if slot == 0:
                    acc[i, :, 128 * h:128 * (h + 1)] = kept
                else:
                    acc[i, :, 128 * h:128 * (h + 1)] += kept

    a_local.wait()
    for slot in (0, 1, 4):
        low(slot, 0, 1)
    z_serve(STREAM_A, 2)
    z_serve(STREAM_A, 3)
    for way in range(2):
        y_tok[way][1].wait_recv()
    for slot in (0, 1, 4):
        low(slot, 1, 3)
    for slot in (2, 5):
        low(slot, 0, 3)
    z_serve(STREAM_A, 4)
    for way in range(2):
        y_tok[way][2].wait_recv()
    for slot in (0, 1, 4, 2, 5):
        low(slot, 3, 4)
    z_serve(STREAM_A, 5)
    low(3, 0, 4)
    z_begin(1, 0, 1)
    low(6, 0, 4)
    z_serve(STREAM_A, 6)
    z_begin(2, 0)

    lane = lax.broadcasted_iota(jnp.int32, (256, 128), 1)

    def folded(i, half):
        rows = slice(256 * half, 256 * (half + 1))
        h = acc[i, rows, 0:128] + acc[i, rows, 128:256]
        return h + pltpu.roll(h, 64, 1)

    def pack(one, other):
        return jnp.where(lane < 64, folded(*one), folded(*other))

    def partial_copies(group):
        return [
            remote(
                packed[group].at[lax.rem(t + k, 8)], part_recv[group].at[k - 1],
                p_send.at[7 * group + k - 1], p_recv.at[7 * group + k - 1], others[k - 1],
            )
            for k in range(1, 8)
        ]

    p_copies = [partial_copies(group) for group in range(2)]

    def add_up(group):
        for copy in p_copies[group]:
            copy.wait_recv()
        total = packed[group][t]
        for k in range(7):
            total += part_recv[group][k]
        low_all[group][t] = total.astype(BF)
        for k in range(1, 8):
            go(remote(
                low_all[group].at[t], low_all[group].at[t],
                g_send.at[7 * group + k - 1], g_recv.at[7 * group + k - 1], others[k - 1],
            ))

    def collect(group):
        for k in range(1, 8):
            remote(
                low_all[group].at[t], low_all[group].at[lax.rem(t + 8 - k, 8)],
                g_send.at[7 * group + k - 1], g_recv.at[7 * group + k - 1], others[k - 1],
            ).wait_recv()

    low(7, 3, 4)
    packed[0][...] = pack((3, 0), (3, 1)).reshape(8, 32, 128)
    for copy in p_copies[0]:
        go(copy)
    z_serve(1, 0)
    low(7, 0, 3)
    z_serve(1, 1)
    z_begin(2, 1)
    pieces = [pack((1, 0), (2, 0)), pack((1, 1), (2, 1)), pack((0, 0), (0, 1))]
    packed[1][...] = jnp.concatenate(pieces, axis=0).reshape(8, 96, 128)
    for copy in p_copies[1]:
        go(copy)
    z_serve(1, 2)
    add_up(0)
    z_serve(1, 3)
    z_serve(2, 0)
    z_serve(1, 4)
    z_serve(2, 1)
    add_up(1)
    z_serve(1, 5)
    z_serve(1, 6)
    collect(0)

    def place(i):
        group, first = (0, 0) if i == 3 else (1, 512 if i == 0 else 0)
        v = low_all[group][...].astype(F32).reshape(-1, 128)[first:first + (512 if i in (1, 2) else 256)]
        turned = pltpu.roll(v, 64, 1)
        if i in (1, 2):
            left = lax.broadcasted_iota(jnp.int32, (512, 128), 1) < 64
            both = jnp.where(left, v, turned) if i == 1 else jnp.where(left, turned, v)
        else:
            both = jnp.concatenate([jnp.where(lane < 64, v, turned), jnp.where(lane < 64, turned, v)], axis=0)
        both = both.astype(BF)
        rows = s_bc[i].astype(BF)
        for slot in range(8):
            for h in range(2):
                want = (first_row(slot) + 2 * h + quarter).astype(BF)
                column = slot * 256 + 128 * h
                spread[i, :, column:column + 128] = jnp.where(rows == want, both, jnp.zeros_like(both))

    for copy in b_local:
        copy.wait()

    def r_copy(n, index, src, dst, way):
        i = n * 6 + index
        return remote(src, dst, r_send.at[i], r_recv.at[i], y_dev[way])

    r_first = [[r_copy(n, w, y_send[n].at[4 + w], y_half[n].at[w], w) for w in range(2)] for n in range(2)]
    r_plain = [
        [r_copy(n, 2 + w, y_send[n].at[2 * (1 - w) + 1 - w], y_recv[n].at[w, 1 - w], w) for w in range(2)]
        for n in range(2)
    ]
    r_added = [
        [r_copy(n, 4 + w, y_send[n].at[2 * (1 - w) + w], y_recv[n].at[w, w], w) for w in range(2)]
        for n in range(2)
    ]

    def adapted(n, i):
        return jnp.dot(spread[i], b_all[n][...], preferred_element_type=F32)

    def to_send(n, i):
        part = adapted(n, i).astype(BF)
        y_send[n][2 * i - 2] = part[0:256]
        y_send[n][2 * i - 1] = part[256:512]

    def send_first(n):
        for way in range(2):
            part = jnp.dot(spread[3, 256 * way:256 * (way + 1)], b_all[n][...], preferred_element_type=F32)
            y_send[n][4 + way] = part.astype(BF)
            go(r_first[n][way])

    def send_plain(n, way):
        to_send(n, 2 - way)
        go(r_plain[n][way])

    def send_added(n):
        for way in range(2):
            r_first[n][way].wait_recv()
            at = 2 * (1 - way) + way
            y_send[n][at] = (y_send[n][at].astype(F32) + y_half[n][way].astype(F32)).astype(BF)
            go(r_added[n][way])

    def mine(n):
        part = adapted(n, 0)
        own_adapted[n][0] = part[0:256]
        own_adapted[n][1] = part[256:512]

    def finish(n):
        for way in range(2):
            r_plain[n][way].wait_recv()
            r_added[n][way].wait_recv()
        first, width = CUTS[n]
        for i in range(2):
            extra = own_adapted[n][i] + (y_recv[n][0, i].astype(F32) + y_recv[n][1, i].astype(F32))
            out_ref[256 * i:256 * (i + 1), first:first + width] = (
                base_own[i, :, first:first + width] + 2.0 * extra
            ).astype(BF)

    place(3)
    send_first(0)
    z_serve(2, 2)
    collect(1)
    place(2)
    send_plain(0, 0)
    z_serve(2, 3)
    place(1)
    send_plain(0, 1)
    z_serve(2, 4)
    send_added(0)
    place(0)
    mine(0)
    for way in range(2):
        x_plain[way].wait_recv()
        x_added[way].wait_recv()
    for i in range(2):
        base_own[i] += x_recv[0, i].astype(F32) + x_recv[1, i].astype(F32)
    z_serve(2, 5)
    z_serve(2, 6)
    send_first(1)
    send_plain(1, 0)
    send_plain(1, 1)
    send_added(1)
    mine(1)
    finish(0)
    finish(1)
    for copy in started:
        copy.wait_send()


def body(
    tokens,
    projection_weight,
    adapter_input_maps,
    adapter_output_maps,
    adapter_store_row,
    adapter_lists_by_batch,
    request_list_position,
):
    dma = pltpu.SemaphoreType.DMA
    vmem = pltpu.VMEM
    hbm = pl.BlockSpec(memory_space=pl.ANY)
    near = pl.BlockSpec(memory_space=pltpu.VMEM)
    return pl.pallas_call(
        kernel,
        out_shape=jax.ShapeDtypeStruct((512, 512), BF),
        in_specs=[hbm] * 4 + [near] * 3,
        out_specs=near,
        scratch_shapes=[
            vmem((4, 512, 1024), BF),
            vmem((8, 256, 1024), BF),
            *[vmem((2048, width), BF) for _, width in CUTS],
            vmem((4, 8, 512), F32),
            vmem((4, 512, 128), F32),
            vmem((8, 1024, 512), BF),
            vmem((4, 512, 256), F32),
            vmem((4, 2, 256, 512), BF),
            vmem((4, 2, 256, 512), BF),
            vmem((3, 2, 256, 512), BF),
            vmem((2, 256, 512), F32),
            vmem((2, 256, 512), BF),
            vmem((2, 2, 256, 512), BF),
            vmem((8, 32, 128), F32),
            vmem((8, 96, 128), F32),
            vmem((7, 32, 128), F32),
            vmem((7, 96, 128), F32),
            vmem((8, 32, 128), BF),
            vmem((8, 96, 128), BF),
            vmem((4, 512, 2048), BF),
            *[
                scratch
                for _, width in CUTS
                for scratch in (
                    vmem((6, 256, width), BF),
                    vmem((2, 256, width), BF),
                    vmem((2, 2, 256, width), BF),
                    vmem((2, 256, width), F32),
                )
            ],
            dma((5,)), dma((8,)), dma((42,)), dma((42,)), dma((6,)), dma((6,)), dma((3,)), dma((3,)),
            dma((4,)), dma((4,)), dma((6,)), dma((6,)), dma((14,)), dma((14,)), dma((14,)), dma((14,)),
            dma((12,)), dma((12,)),
        ],
        compiler_params=pltpu.CompilerParams(
            collective_id=0, has_side_effects=True, vmem_limit_bytes=56 * 1024 * 1024
        ),
        cost_estimate=pl.CostEstimate(flops=17_200_000_000, bytes_accessed=13_000_000, transcendentals=0),
    )(
        tokens,
        projection_weight,
        jnp.swapaxes(adapter_input_maps, 1, 2).reshape(256, 1024),
        adapter_output_maps.reshape(256, 512),
        adapter_store_row.reshape(1, 128),
        adapter_lists_by_batch,
        request_list_position.reshape(1, 512),
    )


def solution(mesh):
    in_specs = (
        P("batch", "tensor"),
        P("tensor", None),
        P("batch", "tensor", None),
        P("batch", None, "tensor"),
        P(),
        P("batch", None),
        P("batch", None),
    )
    out_specs = P("batch", "tensor")
    return jax.shard_map(body, mesh=mesh, in_specs=in_specs, out_specs=out_specs, check_vma=False)
```

```python
import jax
import jax.numpy as jnp
from jax import lax
from jax.experimental import pallas as pl
from jax.experimental.pallas import tpu as pltpu
from jax.sharding import PartitionSpec as P

MESH = pl.DeviceIdType.MESH
BF = jnp.bfloat16
F32 = jnp.float32
NT = (((1,), (1,)), ((), ()))
PLUS, MINUS = 0, 1
STREAM_A = 0
CUTS = ((0, 256), (256, 256))


def kernel(
    tok_h, w_h, a_h, b_h, store_ref, list_ref, pos_ref, out_ref,
    tok_all, a_all, b_all_0, b_all_1, s_all, s_bc, wbuf, acc,
    mate_send, mate_recv, q, base_own, x_half, x_recv,
    packed_0, packed_1, part_0, part_1, low_0, low_1, spread,
    y_send_0, y_half_0, y_recv_0, own_0, y_send_1, y_half_1, y_recv_1, own_1,
    local_sem, w_sem, z_send, z_recv, yt_send, yt_recv, s_send, s_recv,
    m_send, m_recv, x_send_sem, x_recv_sem, p_send, p_recv, g_send, g_recv,
    r_send, r_recv,
):
    b_all = (b_all_0, b_all_1)
    packed, part_recv, low_all = (packed_0, packed_1), (part_0, part_1), (low_0, low_1)
    y_send, y_half = (y_send_0, y_send_1), (y_half_0, y_half_1)
    y_recv, own_adapted = (y_recv_0, y_recv_1), (own_0, own_1)
    b = lax.axis_index("batch")
    t = lax.axis_index("tensor")
    z, y = lax.div(b, 4), lax.rem(b, 4)
    x, c = lax.div(t, 2), lax.rem(t, 2)

    def at_z(d):
        return lax.rem(z + d + 8, 8)

    z_dev = ((at_z(1) * 4 + y, t), (at_z(-1) * 4 + y, t))
    y_dev = ((z * 4 + lax.rem(y + 1, 4), t), (z * 4 + lax.rem(y + 3, 4), t))
    y_far = (z * 4 + lax.rem(y + 2, 4), t)
    x_dev = ((b, lax.rem(x + 1, 4) * 2 + c), (b, lax.rem(x + 3, 4) * 2 + c))
    mate = (b, x * 2 + 1 - c)
    others = [(b, lax.rem(t + k, 8)) for k in range(1, 8)]

    started = []

    def go(copy):
        copy.start()
        started.append(copy)

    def remote(src, dst, send, recv, device):
        return pltpu.make_async_remote_copy(
            src_ref=src, dst_ref=dst, send_sem=send, recv_sem=recv,
            device_id=device, device_id_type=MESH,
        )

    tok_local = [pltpu.make_async_copy(tok_h, tok_all.at[0], local_sem.at[0])]
    a_local = pltpu.make_async_copy(a_h, a_all.at[0], local_sem.at[2])
    b_local = [
        pltpu.make_async_copy(
            b_h.at[:, pl.ds(*CUTS[n])], b_all[n].at[pl.ds(0, 256)], local_sem.at[3 + n]
        )
        for n in range(2)
    ]
    chips = [lax.rem(x + d, 4) for d in (2, 1, 3, 0)]
    w_local = []
    for j in range(8):
        column = (chips[j % 4] * 2 + (1 - c if j < 4 else c)) * 512
        w_local.append(
            pltpu.make_async_copy(
                w_h.at[:, pl.ds(pl.multiple_of(column, 512), 512)], wbuf.at[j], w_sem.at[j]
            )
        )
    for copy in tok_local + w_local[:2] + [a_local] + w_local[2:] + b_local:
        copy.start()

    barrier = pltpu.get_barrier_semaphore()
    partners = [z_dev[0], z_dev[1], y_dev[0], y_dev[1], y_far] + others
    for device in partners:
        pl.semaphore_signal(barrier, inc=1, device_id=device, device_id_type=MESH)

    list_row = jnp.broadcast_to(list_ref[...].astype(F32), (32, 32))
    eye = lax.broadcasted_iota(jnp.int32, (32, 32), 0) == lax.broadcasted_iota(jnp.int32, (32, 32), 1)
    list_col = jnp.sum(jnp.where(eye, list_row, 0.0), axis=1, keepdims=True)
    lane_a = lax.broadcasted_iota(jnp.int32, (32, 128), 1).astype(F32)
    rows_col = jnp.sum(
        jnp.where(lane_a == list_col, jnp.broadcast_to(store_ref[...].astype(F32), (32, 128)), 0.0),
        axis=1, keepdims=True,
    )
    hot = lax.broadcasted_iota(jnp.int32, (32, 512), 0) == jnp.broadcast_to(pos_ref[...], (32, 512))
    s_row = jnp.sum(jnp.where(hot, jnp.broadcast_to(rows_col, (32, 512)), 0.0), axis=0, keepdims=True)
    s_all[0] = jnp.broadcast_to(s_row, (8, 512))

    pl.semaphore_wait(barrier, len(partners))

    s_copies = [
        remote(s_all.at[0], s_all.at[slot], s_send.at[slot - 1], s_recv.at[slot - 1], device)
        for slot, device in ((1, y_dev[0]), (2, y_dev[1]), (3, y_far))
    ]

    def z_rows(way, k):
        return k // 2 + 1, ((k % 2) ^ way) * 128, 128

    def z_place(stream, slot, row, rows):
        if stream == STREAM_A:
            return a_all.at[slot, pl.ds(row, rows)]
        return b_all[stream - 1].at[pl.ds(slot * 256 + row, rows)]

    def z_own(stream, row, rows):
        if stream == STREAM_A:
            return a_h.at[pl.ds(row, rows)]
        return b_h.at[pl.ds(row, rows), pl.ds(*CUTS[stream - 1])]

    def z_slot(way, d):
        return 7 if d == 4 else d + 3 * way

    def z_copy(stream, way, k):
        d, row, rows = z_rows(way, k)
        src = z_own(stream, row, rows) if d == 1 else z_place(stream, z_slot(way, d - 1), row, rows)
        i = stream * 14 + way * 7 + k
        return remote(
            src, z_place(stream, z_slot(way, d), row, rows), z_send.at[i], z_recv.at[i], z_dev[way]
        )

    z_all = [[[z_copy(s, w, k) for k in range(7)] for w in range(2)] for s in range(3)]

    def z_begin(stream, *steps):
        for k in steps:
            for way in range(2):
                go(z_all[stream][way][k])

    def z_serve(stream, k):
        for way in range(2):
            z_all[stream][way][k].wait_recv()
            if k < 5:
                go(z_all[stream][way][k + 2])

    def y_copy(way, k):
        rows = pl.ds(256 * ((k % 2) ^ way), 256)
        if k < 2:
            src, dst = tok_h.at[rows], tok_all.at[1 + way, rows]
        else:
            src, dst = tok_all.at[1 + way, rows], tok_all.at[3, rows]
        return remote(src, dst, yt_send.at[way * 3 + k], yt_recv.at[way * 3 + k], y_dev[way])

    y_tok = [[y_copy(w, k) for k in range(3)] for w in range(2)]

    z_begin(STREAM_A, 0, 1)
    for copy in s_copies:
        go(copy)
    for k in range(2):
        for way in range(2):
            go(y_tok[way][k])

    for copy in tok_local:
        copy.wait()

    mate_copies = [
        remote(mate_send.at[j], mate_recv.at[j], m_send.at[j], m_recv.at[j], mate) for j in range(4)
    ]

    def base_part(j):
        return jnp.dot(tok_all[0], wbuf[j], preferred_element_type=F32)

    for j in range(4):
        w_local[j].wait()

        part = base_part(j).astype(BF)
        mate_send[j, 0] = part[0:256]
        mate_send[j, 1] = part[256:512]

        go(mate_copies[j])

    def base_mine(j):
        w_local[4 + j].wait()
        mate_copies[j].wait_recv()

        part = base_part(4 + j)
        for i in range(2):
            total = part[256 * i:256 * (i + 1)] + mate_recv[j, i].astype(F32)
            if j < 3:
                q[j, i] = total.astype(BF)
            else:
                base_own[i] = total

    def x_copy(n, src, dst, way):
        return remote(src, dst, x_send_sem.at[n], x_recv_sem.at[n], x_dev[way])

    x_first = [x_copy(w, q.at[0, w], x_half.at[w], w) for w in range(2)]
    x_plain = [x_copy(2 + w, q.at[1 + w, 1 - w], x_recv.at[w, 1 - w], w) for w in range(2)]
    x_added = [x_copy(4 + w, q.at[1 + w, w], x_recv.at[w, w], w) for w in range(2)]

    base_mine(0)
    for copy in x_first:
        go(copy)
    base_mine(1)
    go(x_plain[0])
    base_mine(2)
    go(x_plain[1])
    z_serve(STREAM_A, 0)
    base_mine(3)

    for copy in s_copies:
        copy.wait_recv()
    for slot in range(4):
        for block in range(4):
            row = s_all[slot, 0:1, 128 * block:128 * (block + 1)]
            tile = jnp.broadcast_to(row, (128, 128)).T
            s_bc[slot, 128 * block:128 * (block + 1)] = tile

    z_serve(STREAM_A, 1)
    for way in range(2):
        y_tok[way][0].wait_recv()
        go(y_tok[way][2])
    for way in range(2):
        x_first[way].wait_recv()
        q[1 + way, way] = (q[1 + way, way].astype(F32) + x_half[way].astype(F32)).astype(BF)
        go(x_added[way])

    quarter = lax.broadcasted_iota(jnp.int32, (512, 128), 1) // 64

    def first_row(slot):
        d = 4 if slot == 7 else (-slot if slot < 4 else slot - 3)
        return at_z(d) * 16 + y * 4

    def low(slot, lowest, highest):
        rows = [(first_row(slot) + 2 * h + quarter).astype(F32) for h in range(2)]

        @pl.loop(lowest, highest)
        def _(i):
            product = lax.dot_general(tok_all[i], a_all[slot], NT, preferred_element_type=F32)
            for h in range(2):
                kept = jnp.where(s_bc[i] == rows[h], product[:, 128 * h:128 * (h + 1)], 0.0)
                if slot == 0:
                    acc[i, :, 128 * h:128 * (h + 1)] = kept
                else:
                    acc[i, :, 128 * h:128 * (h + 1)] += kept

    a_local.wait()
    for slot in (0, 1, 4):
        low(slot, 0, 1)
    z_serve(STREAM_A, 2)
    z_serve(STREAM_A, 3)
    for way in range(2):
        y_tok[way][1].wait_recv()
    for slot in (0, 1, 4):
        low(slot, 1, 3)
    for slot in (2, 5):
        low(slot, 0, 3)
    z_serve(STREAM_A, 4)
    for way in range(2):
        y_tok[way][2].wait_recv()
    for slot in (0, 1, 4, 2, 5):
        low(slot, 3, 4)
    z_begin(1, 0, 1)
    z_serve(STREAM_A, 5)
    low(3, 0, 4)
    z_begin(2, 0)
    low(6, 0, 4)
    z_serve(STREAM_A, 6)

    lane = lax.broadcasted_iota(jnp.int32, (256, 128), 1)

    def folded(i, half):
        rows = slice(256 * half, 256 * (half + 1))
        h = acc[i, rows, 0:128] + acc[i, rows, 128:256]
        return h + pltpu.roll(h, 64, 1)

    def pack(one, other):
        return jnp.where(lane < 64, folded(*one), folded(*other))

    def partial_copies(group):
        return [
            remote(
                packed[group].at[lax.rem(t + k, 8)], part_recv[group].at[k - 1],
                p_send.at[7 * group + k - 1], p_recv.at[7 * group + k - 1], others[k - 1],
            )
            for k in range(1, 8)
        ]

    p_copies = [partial_copies(group) for group in range(2)]

    def add_up(group):
        for copy in p_copies[group]:
            copy.wait_recv()
        total = packed[group][t]
        for k in range(7):
            total += part_recv[group][k]
        low_all[group][t] = total.astype(BF)
        for k in range(1, 8):
            go(remote(
                low_all[group].at[t], low_all[group].at[t],
                g_send.at[7 * group + k - 1], g_recv.at[7 * group + k - 1], others[k - 1],
            ))

    def collect(group):
        for k in range(1, 8):
            remote(
                low_all[group].at[t], low_all[group].at[lax.rem(t + 8 - k, 8)],
                g_send.at[7 * group + k - 1], g_recv.at[7 * group + k - 1], others[k - 1],
            ).wait_recv()

    low(7, 3, 4)
    packed[0][...] = pack((3, 0), (3, 1)).reshape(8, 32, 128)
    for copy in p_copies[0]:
        go(copy)
    z_serve(1, 0)
    low(7, 0, 3)
    z_serve(1, 1)
    z_begin(2, 1)
    pieces = [pack((1, 0), (2, 0)), pack((1, 1), (2, 1)), pack((0, 0), (0, 1))]
    packed[1][...] = jnp.concatenate(pieces, axis=0).reshape(8, 96, 128)
    for copy in p_copies[1]:
        go(copy)
    z_serve(1, 2)
    add_up(0)
    z_serve(1, 3)
    z_serve(2, 0)
    z_serve(1, 4)
    z_serve(2, 1)
    add_up(1)
    z_serve(1, 5)
    z_serve(2, 2)
    z_serve(1, 6)
    collect(0)

    def place(i):
        group, first = (0, 0) if i == 3 else (1, 512 if i == 0 else 0)
        v = low_all[group][...].astype(F32).reshape(-1, 128)[first:first + (512 if i in (1, 2) else 256)]
        turned = pltpu.roll(v, 64, 1)
        if i in (1, 2):
            left = lax.broadcasted_iota(jnp.int32, (512, 128), 1) < 64
            both = jnp.where(left, v, turned) if i == 1 else jnp.where(left, turned, v)
        else:
            both = jnp.concatenate([jnp.where(lane < 64, v, turned), jnp.where(lane < 64, turned, v)], axis=0)
        both = both.astype(BF)
        rows = s_bc[i].astype(BF)
        for slot in range(8):
            for h in range(2):
                want = (first_row(slot) + 2 * h + quarter).astype(BF)
                column = slot * 256 + 128 * h
                spread[i, :, column:column + 128] = jnp.where(rows == want, both, jnp.zeros_like(both))

    for copy in b_local:
        copy.wait()

    def r_copy(n, index, src, dst, way):
        i = n * 6 + index
        return remote(src, dst, r_send.at[i], r_recv.at[i], y_dev[way])

    r_first = [[r_copy(n, w, y_send[n].at[4 + w], y_half[n].at[w], w) for w in range(2)] for n in range(2)]
    r_plain = [
        [r_copy(n, 2 + w, y_send[n].at[2 * (1 - w) + 1 - w], y_recv[n].at[w, 1 - w], w) for w in range(2)]
        for n in range(2)
    ]
    r_added = [
        [r_copy(n, 4 + w, y_send[n].at[2 * (1 - w) + w], y_recv[n].at[w, w], w) for w in range(2)]
        for n in range(2)
    ]

    def adapted(n, i):
        return jnp.dot(spread[i], b_all[n][...], preferred_element_type=F32)

    def to_send(n, i):
        part = adapted(n, i).astype(BF)
        y_send[n][2 * i - 2] = part[0:256]
        y_send[n][2 * i - 1] = part[256:512]

    def send_first(n):
        for way in range(2):
            part = jnp.dot(spread[3, 256 * way:256 * (way + 1)], b_all[n][...], preferred_element_type=F32)
            y_send[n][4 + way] = part.astype(BF)
            go(r_first[n][way])

    def send_plain(n, way):
        to_send(n, 2 - way)
        go(r_plain[n][way])

    def send_added(n):
        for way in range(2):
            r_first[n][way].wait_recv()
            at = 2 * (1 - way) + way
            y_send[n][at] = (y_send[n][at].astype(F32) + y_half[n][way].astype(F32)).astype(BF)
            go(r_added[n][way])

    def mine(n):
        part = adapted(n, 0)
        own_adapted[n][0] = part[0:256]
        own_adapted[n][1] = part[256:512]

    def finish(n):
        for way in range(2):
            r_plain[n][way].wait_recv()
            r_added[n][way].wait_recv()
        first, width = CUTS[n]
        for i in range(2):
            extra = own_adapted[n][i] + (y_recv[n][0, i].astype(F32) + y_recv[n][1, i].astype(F32))
            out_ref[256 * i:256 * (i + 1), first:first + width] = (
                base_own[i, :, first:first + width] + 2.0 * extra
            ).astype(BF)

    place(3)
    send_first(0)
    z_serve(2, 3)
    collect(1)
    place(2)
    send_plain(0, 0)
    z_serve(2, 4)
    place(1)
    send_plain(0, 1)
    send_added(0)
    place(0)
    mine(0)
    for way in range(2):
        x_plain[way].wait_recv()
        x_added[way].wait_recv()
    for i in range(2):
        base_own[i] += x_recv[0, i].astype(F32) + x_recv[1, i].astype(F32)
    z_serve(2, 5)
    z_serve(2, 6)
    send_first(1)
    send_plain(1, 0)
    send_plain(1, 1)
    send_added(1)
    mine(1)
    finish(0)
    finish(1)
    for copy in started:
        copy.wait_send()


def body(
    tokens,
    projection_weight,
    adapter_input_maps,
    adapter_output_maps,
    adapter_store_row,
    adapter_lists_by_batch,
    request_list_position,
):
    dma = pltpu.SemaphoreType.DMA
    vmem = pltpu.VMEM
    hbm = pl.BlockSpec(memory_space=pl.ANY)
    near = pl.BlockSpec(memory_space=pltpu.VMEM)
    return pl.pallas_call(
        kernel,
        out_shape=jax.ShapeDtypeStruct((512, 512), BF),
        in_specs=[hbm] * 4 + [near] * 3,
        out_specs=near,
        scratch_shapes=[
            vmem((4, 512, 1024), BF),
            vmem((8, 256, 1024), BF),
            *[vmem((2048, width), BF) for _, width in CUTS],
            vmem((4, 8, 512), F32),
            vmem((4, 512, 128), F32),
            vmem((8, 1024, 512), BF),
            vmem((4, 512, 256), F32),
            vmem((4, 2, 256, 512), BF),
            vmem((4, 2, 256, 512), BF),
            vmem((3, 2, 256, 512), BF),
            vmem((2, 256, 512), F32),
            vmem((2, 256, 512), BF),
            vmem((2, 2, 256, 512), BF),
            vmem((8, 32, 128), F32),
            vmem((8, 96, 128), F32),
            vmem((7, 32, 128), F32),
            vmem((7, 96, 128), F32),
            vmem((8, 32, 128), BF),
            vmem((8, 96, 128), BF),
            vmem((4, 512, 2048), BF),
            *[
                scratch
                for _, width in CUTS
                for scratch in (
                    vmem((6, 256, width), BF),
                    vmem((2, 256, width), BF),
                    vmem((2, 2, 256, width), BF),
                    vmem((2, 256, width), F32),
                )
            ],
            dma((5,)), dma((8,)), dma((42,)), dma((42,)), dma((6,)), dma((6,)), dma((3,)), dma((3,)),
            dma((4,)), dma((4,)), dma((6,)), dma((6,)), dma((14,)), dma((14,)), dma((14,)), dma((14,)),
            dma((12,)), dma((12,)),
        ],
        compiler_params=pltpu.CompilerParams(
            collective_id=0, has_side_effects=True, vmem_limit_bytes=56 * 1024 * 1024
        ),
        cost_estimate=pl.CostEstimate(flops=17_200_000_000, bytes_accessed=13_000_000, transcendentals=0),
    )(
        tokens,
        projection_weight,
        jnp.swapaxes(adapter_input_maps, 1, 2).reshape(256, 1024),
        adapter_output_maps.reshape(256, 512),
        adapter_store_row.reshape(1, 128),
        adapter_lists_by_batch,
        request_list_position.reshape(1, 512),
    )


def solution(mesh):
    in_specs = (
        P("batch", "tensor"),
        P("tensor", None),
        P("batch", "tensor", None),
        P("batch", None, "tensor"),
        P(),
        P("batch", None),
        P("batch", None),
    )
    out_specs = P("batch", "tensor")
    return jax.shard_map(body, mesh=mesh, in_specs=in_specs, out_specs=out_specs, check_vma=False)
```

```python
import jax
import jax.numpy as jnp
from jax import lax
from jax.experimental import pallas as pl
from jax.experimental.pallas import tpu as pltpu
from jax.sharding import PartitionSpec as P

MESH = pl.DeviceIdType.MESH
BF = jnp.bfloat16
F32 = jnp.float32
NT = (((1,), (1,)), ((), ()))
PLUS, MINUS = 0, 1
STREAM_A = 0
CUTS = ((0, 256), (256, 256))


def kernel(
    tok_h, w_h, a_h, b_h, store_ref, list_ref, pos_ref, out_ref,
    tok_all, a_all, b_all_0, b_all_1, s_all, s_bc, wbuf, acc,
    mate_send, mate_recv, q, base_own, x_half, x_recv,
    packed_0, packed_1, part_0, part_1, low_0, low_1, spread,
    y_send_0, y_half_0, y_recv_0, own_0, y_send_1, y_half_1, y_recv_1, own_1,
    local_sem, w_sem, z_send, z_recv, yt_send, yt_recv, s_send, s_recv,
    m_send, m_recv, x_send_sem, x_recv_sem, p_send, p_recv, g_send, g_recv,
    r_send, r_recv,
):
    b_all = (b_all_0, b_all_1)
    packed, part_recv, low_all = (packed_0, packed_1), (part_0, part_1), (low_0, low_1)
    y_send, y_half = (y_send_0, y_send_1), (y_half_0, y_half_1)
    y_recv, own_adapted = (y_recv_0, y_recv_1), (own_0, own_1)
    b = lax.axis_index("batch")
    t = lax.axis_index("tensor")
    z, y = lax.div(b, 4), lax.rem(b, 4)
    x, c = lax.div(t, 2), lax.rem(t, 2)

    def at_z(d):
        return lax.rem(z + d + 8, 8)

    z_dev = ((at_z(1) * 4 + y, t), (at_z(-1) * 4 + y, t))
    y_dev = ((z * 4 + lax.rem(y + 1, 4), t), (z * 4 + lax.rem(y + 3, 4), t))
    y_far = (z * 4 + lax.rem(y + 2, 4), t)
    x_dev = ((b, lax.rem(x + 1, 4) * 2 + c), (b, lax.rem(x + 3, 4) * 2 + c))
    mate = (b, x * 2 + 1 - c)
    others = [(b, lax.rem(t + k, 8)) for k in range(1, 8)]

    started = []

    def go(copy):
        copy.start()
        started.append(copy)

    def remote(src, dst, send, recv, device):
        return pltpu.make_async_remote_copy(
            src_ref=src, dst_ref=dst, send_sem=send, recv_sem=recv,
            device_id=device, device_id_type=MESH,
        )

    tok_local = [pltpu.make_async_copy(tok_h, tok_all.at[0], local_sem.at[0])]
    a_local = pltpu.make_async_copy(a_h, a_all.at[0], local_sem.at[2])
    b_local = [
        pltpu.make_async_copy(
            b_h.at[:, pl.ds(*CUTS[n])], b_all[n].at[pl.ds(0, 256)], local_sem.at[3 + n]
        )
        for n in range(2)
    ]
    chips = [lax.rem(x + d, 4) for d in (2, 1, 3, 0)]
    w_local = []
    for j in range(8):
        column = (chips[j % 4] * 2 + (1 - c if j < 4 else c)) * 512
        w_local.append(
            pltpu.make_async_copy(
                w_h.at[:, pl.ds(pl.multiple_of(column, 512), 512)], wbuf.at[j], w_sem.at[j]
            )
        )
    for copy in tok_local + w_local[:2] + [a_local] + w_local[2:] + b_local:
        copy.start()

    barrier = pltpu.get_barrier_semaphore()
    partners = [z_dev[0], z_dev[1], y_dev[0], y_dev[1], y_far] + others
    for device in partners:
        pl.semaphore_signal(barrier, inc=1, device_id=device, device_id_type=MESH)

    list_row = jnp.broadcast_to(list_ref[...].astype(F32), (32, 32))
    eye = lax.broadcasted_iota(jnp.int32, (32, 32), 0) == lax.broadcasted_iota(jnp.int32, (32, 32), 1)
    list_col = jnp.sum(jnp.where(eye, list_row, 0.0), axis=1, keepdims=True)
    lane_a = lax.broadcasted_iota(jnp.int32, (32, 128), 1).astype(F32)
    rows_col = jnp.sum(
        jnp.where(lane_a == list_col, jnp.broadcast_to(store_ref[...].astype(F32), (32, 128)), 0.0),
        axis=1, keepdims=True,
    )
    hot = lax.broadcasted_iota(jnp.int32, (32, 512), 0) == jnp.broadcast_to(pos_ref[...], (32, 512))
    s_row = jnp.sum(jnp.where(hot, jnp.broadcast_to(rows_col, (32, 512)), 0.0), axis=0, keepdims=True)
    s_all[0] = jnp.broadcast_to(s_row, (8, 512))

    pl.semaphore_wait(barrier, len(partners))

    s_copies = [
        remote(s_all.at[0], s_all.at[slot], s_send.at[slot - 1], s_recv.at[slot - 1], device)
        for slot, device in ((1, y_dev[0]), (2, y_dev[1]), (3, y_far))
    ]

    def z_rows(way, k):
        return k // 2 + 1, ((k % 2) ^ way) * 128, 128

    def z_place(stream, slot, row, rows):
        if stream == STREAM_A:
            return a_all.at[slot, pl.ds(row, rows)]
        return b_all[stream - 1].at[pl.ds(slot * 256 + row, rows)]

    def z_own(stream, row, rows):
        if stream == STREAM_A:
            return a_h.at[pl.ds(row, rows)]
        return b_h.at[pl.ds(row, rows), pl.ds(*CUTS[stream - 1])]

    def z_slot(way, d):
        return 7 if d == 4 else d + 3 * way

    def z_copy(stream, way, k):
        d, row, rows = z_rows(way, k)
        src = z_own(stream, row, rows) if d == 1 else z_place(stream, z_slot(way, d - 1), row, rows)
        i = stream * 14 + way * 7 + k
        return remote(
            src, z_place(stream, z_slot(way, d), row, rows), z_send.at[i], z_recv.at[i], z_dev[way]
        )

    z_all = [[[z_copy(s, w, k) for k in range(7)] for w in range(2)] for s in range(3)]

    def z_begin(stream, *steps):
        for k in steps:
            for way in range(2):
                go(z_all[stream][way][k])

    def z_serve(stream, k):
        for way in range(2):
            z_all[stream][way][k].wait_recv()
            if k < 5:
                go(z_all[stream][way][k + 2])

    def y_copy(way, k):
        rows = pl.ds(256 * ((k % 2) ^ way), 256)
        if k < 2:
            src, dst = tok_h.at[rows], tok_all.at[1 + way, rows]
        else:
            src, dst = tok_all.at[1 + way, rows], tok_all.at[3, rows]
        return remote(src, dst, yt_send.at[way * 3 + k], yt_recv.at[way * 3 + k], y_dev[way])

    y_tok = [[y_copy(w, k) for k in range(3)] for w in range(2)]

    z_begin(STREAM_A, 0, 1)
    for copy in s_copies:
        go(copy)
    for k in range(2):
        for way in range(2):
            go(y_tok[way][k])

    for copy in tok_local:
        copy.wait()

    mate_copies = [
        remote(mate_send.at[j], mate_recv.at[j], m_send.at[j], m_recv.at[j], mate) for j in range(4)
    ]

    def base_part(j):
        return jnp.dot(tok_all[0], wbuf[j], preferred_element_type=F32)

    for j in range(4):
        w_local[j].wait()

        part = base_part(j).astype(BF)
        mate_send[j, 0] = part[0:256]
        mate_send[j, 1] = part[256:512]

        go(mate_copies[j])

    def base_mine(j):
        w_local[4 + j].wait()
        mate_copies[j].wait_recv()

        part = base_part(4 + j)
        for i in range(2):
            total = part[256 * i:256 * (i + 1)] + mate_recv[j, i].astype(F32)
            if j < 3:
                q[j, i] = total.astype(BF)
            else:
                base_own[i] = total

    def x_copy(n, src, dst, way):
        return remote(src, dst, x_send_sem.at[n], x_recv_sem.at[n], x_dev[way])

    x_first = [x_copy(w, q.at[0, w], x_half.at[w], w) for w in range(2)]
    x_plain = [x_copy(2 + w, q.at[1 + w, 1 - w], x_recv.at[w, 1 - w], w) for w in range(2)]
    x_added = [x_copy(4 + w, q.at[1 + w, w], x_recv.at[w, w], w) for w in range(2)]

    base_mine(0)
    for copy in x_first:
        go(copy)
    base_mine(1)
    go(x_plain[0])
    base_mine(2)
    go(x_plain[1])
    z_serve(STREAM_A, 0)
    base_mine(3)

    for copy in s_copies:
        copy.wait_recv()
    for slot in range(4):
        for block in range(4):
            row = s_all[slot, 0:1, 128 * block:128 * (block + 1)]
            tile = jnp.broadcast_to(row, (128, 128)).T
            s_bc[slot, 128 * block:128 * (block + 1)] = tile

    z_serve(STREAM_A, 1)
    for way in range(2):
        y_tok[way][0].wait_recv()
        go(y_tok[way][2])
    for way in range(2):
        x_first[way].wait_recv()
        q[1 + way, way] = (q[1 + way, way].astype(F32) + x_half[way].astype(F32)).astype(BF)
        go(x_added[way])

    quarter = lax.broadcasted_iota(jnp.int32, (512, 128), 1) // 64

    def first_row(slot):
        d = 4 if slot == 7 else (-slot if slot < 4 else slot - 3)
        return at_z(d) * 16 + y * 4

    def low(slot, lowest, highest):
        rows = [(first_row(slot) + 2 * h + quarter).astype(F32) for h in range(2)]

        @pl.loop(lowest, highest)
        def _(i):
            product = lax.dot_general(tok_all[i], a_all[slot], NT, preferred_element_type=F32)
            for h in range(2):
                kept = jnp.where(s_bc[i] == rows[h], product[:, 128 * h:128 * (h + 1)], 0.0)
                if slot == 0:
                    acc[i, :, 128 * h:128 * (h + 1)] = kept
                else:
                    acc[i, :, 128 * h:128 * (h + 1)] += kept

    a_local.wait()
    for slot in (0, 1, 4):
        low(slot, 0, 1)
    z_serve(STREAM_A, 2)
    z_serve(STREAM_A, 3)
    for way in range(2):
        y_tok[way][1].wait_recv()
    for slot in (0, 1, 4):
        low(slot, 1, 3)
    for slot in (2, 5):
        low(slot, 0, 3)
    z_serve(STREAM_A, 4)
    z_begin(1, 0, 1)
    for way in range(2):
        y_tok[way][2].wait_recv()
    for slot in (0, 1, 4, 2, 5):
        low(slot, 3, 4)
    z_serve(STREAM_A, 5)
    low(3, 0, 4)
    z_begin(2, 0)
    low(6, 0, 4)
    z_serve(STREAM_A, 6)

    lane = lax.broadcasted_iota(jnp.int32, (256, 128), 1)

    def folded(i, half):
        rows = slice(256 * half, 256 * (half + 1))
        h = acc[i, rows, 0:128] + acc[i, rows, 128:256]
        return h + pltpu.roll(h, 64, 1)

    def pack(one, other):
        return jnp.where(lane < 64, folded(*one), folded(*other))

    def partial_copies(group):
        return [
            remote(
                packed[group].at[lax.rem(t + k, 8)], part_recv[group].at[k - 1],
                p_send.at[7 * group + k - 1], p_recv.at[7 * group + k - 1], others[k - 1],
            )
            for k in range(1, 8)
        ]

    p_copies = [partial_copies(group) for group in range(2)]

    def add_up(group):
        for copy in p_copies[group]:
            copy.wait_recv()
        total = packed[group][t]
        for k in range(7):
            total += part_recv[group][k]
        low_all[group][t] = total.astype(BF)
        for k in range(1, 8):
            go(remote(
                low_all[group].at[t], low_all[group].at[t],
                g_send.at[7 * group + k - 1], g_recv.at[7 * group + k - 1], others[k - 1],
            ))

    def collect(group):
        for k in range(1, 8):
            remote(
                low_all[group].at[t], low_all[group].at[lax.rem(t + 8 - k, 8)],
                g_send.at[7 * group + k - 1], g_recv.at[7 * group + k - 1], others[k - 1],
            ).wait_recv()

    low(7, 3, 4)
    packed[0][...] = pack((3, 0), (3, 1)).reshape(8, 32, 128)
    for copy in p_copies[0]:
        go(copy)
    z_serve(1, 0)
    low(7, 0, 3)
    z_serve(1, 1)
    z_begin(2, 1)
    pieces = [pack((1, 0), (2, 0)), pack((1, 1), (2, 1)), pack((0, 0), (0, 1))]
    packed[1][...] = jnp.concatenate(pieces, axis=0).reshape(8, 96, 128)
    for copy in p_copies[1]:
        go(copy)
    z_serve(1, 2)
    add_up(0)
    z_serve(1, 3)
    z_serve(2, 0)
    z_serve(1, 4)
    z_serve(2, 1)
    add_up(1)
    z_serve(1, 5)
    z_serve(2, 2)
    z_serve(1, 6)
    collect(0)

    def place(i):
        group, first = (0, 0) if i == 3 else (1, 512 if i == 0 else 0)
        v = low_all[group][...].astype(F32).reshape(-1, 128)[first:first + (512 if i in (1, 2) else 256)]
        turned = pltpu.roll(v, 64, 1)
        if i in (1, 2):
            left = lax.broadcasted_iota(jnp.int32, (512, 128), 1) < 64
            both = jnp.where(left, v, turned) if i == 1 else jnp.where(left, turned, v)
        else:
            both = jnp.concatenate([jnp.where(lane < 64, v, turned), jnp.where(lane < 64, turned, v)], axis=0)
        both = both.astype(BF)
        rows = s_bc[i].astype(BF)
        for slot in range(8):
            for h in range(2):
                want = (first_row(slot) + 2 * h + quarter).astype(BF)
                column = slot * 256 + 128 * h
                spread[i, :, column:column + 128] = jnp.where(rows == want, both, jnp.zeros_like(both))

    for copy in b_local:
        copy.wait()

    def r_copy(n, index, src, dst, way):
        i = n * 6 + index
        return remote(src, dst, r_send.at[i], r_recv.at[i], y_dev[way])

    r_first = [[r_copy(n, w, y_send[n].at[4 + w], y_half[n].at[w], w) for w in range(2)] for n in range(2)]
    r_plain = [
        [r_copy(n, 2 + w, y_send[n].at[2 * (1 - w) + 1 - w], y_recv[n].at[w, 1 - w], w) for w in range(2)]
        for n in range(2)
    ]
    r_added = [
        [r_copy(n, 4 + w, y_send[n].at[2 * (1 - w) + w], y_recv[n].at[w, w], w) for w in range(2)]
        for n in range(2)
    ]

    def adapted(n, i):
        return jnp.dot(spread[i], b_all[n][...], preferred_element_type=F32)

    def to_send(n, i):
        part = adapted(n, i).astype(BF)
        y_send[n][2 * i - 2] = part[0:256]
        y_send[n][2 * i - 1] = part[256:512]

    def send_first(n):
        for way in range(2):
            part = jnp.dot(spread[3, 256 * way:256 * (way + 1)], b_all[n][...], preferred_element_type=F32)
            y_send[n][4 + way] = part.astype(BF)
            go(r_first[n][way])

    def send_plain(n, way):
        to_send(n, 2 - way)
        go(r_plain[n][way])

    def send_added(n):
        for way in range(2):
            r_first[n][way].wait_recv()
            at = 2 * (1 - way) + way
            y_send[n][at] = (y_send[n][at].astype(F32) + y_half[n][way].astype(F32)).astype(BF)
            go(r_added[n][way])

    def mine(n):
        part = adapted(n, 0)
        own_adapted[n][0] = part[0:256]
        own_adapted[n][1] = part[256:512]

    def finish(n):
        for way in range(2):
            r_plain[n][way].wait_recv()
            r_added[n][way].wait_recv()
        first, width = CUTS[n]
        for i in range(2):
            extra = own_adapted[n][i] + (y_recv[n][0, i].astype(F32) + y_recv[n][1, i].astype(F32))
            out_ref[256 * i:256 * (i + 1), first:first + width] = (
                base_own[i, :, first:first + width] + 2.0 * extra
            ).astype(BF)

    place(3)
    send_first(0)
    z_serve(2, 3)
    collect(1)
    place(2)
    send_plain(0, 0)
    z_serve(2, 4)
    place(1)
    send_plain(0, 1)
    send_added(0)
    place(0)
    mine(0)
    for way in range(2):
        x_plain[way].wait_recv()
        x_added[way].wait_recv()
    for i in range(2):
        base_own[i] += x_recv[0, i].astype(F32) + x_recv[1, i].astype(F32)
    z_serve(2, 5)
    z_serve(2, 6)
    send_first(1)
    send_plain(1, 0)
    send_plain(1, 1)
    send_added(1)
    mine(1)
    finish(0)
    finish(1)
    for copy in started:
        copy.wait_send()


def body(
    tokens,
    projection_weight,
    adapter_input_maps,
    adapter_output_maps,
    adapter_store_row,
    adapter_lists_by_batch,
    request_list_position,
):
    dma = pltpu.SemaphoreType.DMA
    vmem = pltpu.VMEM
    hbm = pl.BlockSpec(memory_space=pl.ANY)
    near = pl.BlockSpec(memory_space=pltpu.VMEM)
    return pl.pallas_call(
        kernel,
        out_shape=jax.ShapeDtypeStruct((512, 512), BF),
        in_specs=[hbm] * 4 + [near] * 3,
        out_specs=near,
        scratch_shapes=[
            vmem((4, 512, 1024), BF),
            vmem((8, 256, 1024), BF),
            *[vmem((2048, width), BF) for _, width in CUTS],
            vmem((4, 8, 512), F32),
            vmem((4, 512, 128), F32),
            vmem((8, 1024, 512), BF),
            vmem((4, 512, 256), F32),
            vmem((4, 2, 256, 512), BF),
            vmem((4, 2, 256, 512), BF),
            vmem((3, 2, 256, 512), BF),
            vmem((2, 256, 512), F32),
            vmem((2, 256, 512), BF),
            vmem((2, 2, 256, 512), BF),
            vmem((8, 32, 128), F32),
            vmem((8, 96, 128), F32),
            vmem((7, 32, 128), F32),
            vmem((7, 96, 128), F32),
            vmem((8, 32, 128), BF),
            vmem((8, 96, 128), BF),
            vmem((4, 512, 2048), BF),
            *[
                scratch
                for _, width in CUTS
                for scratch in (
                    vmem((6, 256, width), BF),
                    vmem((2, 256, width), BF),
                    vmem((2, 2, 256, width), BF),
                    vmem((2, 256, width), F32),
                )
            ],
            dma((5,)), dma((8,)), dma((42,)), dma((42,)), dma((6,)), dma((6,)), dma((3,)), dma((3,)),
            dma((4,)), dma((4,)), dma((6,)), dma((6,)), dma((14,)), dma((14,)), dma((14,)), dma((14,)),
            dma((12,)), dma((12,)),
        ],
        compiler_params=pltpu.CompilerParams(
            collective_id=0, has_side_effects=True, vmem_limit_bytes=56 * 1024 * 1024
        ),
        cost_estimate=pl.CostEstimate(flops=17_200_000_000, bytes_accessed=13_000_000, transcendentals=0),
    )(
        tokens,
        projection_weight,
        jnp.swapaxes(adapter_input_maps, 1, 2).reshape(256, 1024),
        adapter_output_maps.reshape(256, 512),
        adapter_store_row.reshape(1, 128),
        adapter_lists_by_batch,
        request_list_position.reshape(1, 512),
    )


def solution(mesh):
    in_specs = (
        P("batch", "tensor"),
        P("tensor", None),
        P("batch", "tensor", None),
        P("batch", None, "tensor"),
        P(),
        P("batch", None),
        P("batch", None),
    )
    out_specs = P("batch", "tensor")
    return jax.shard_map(body, mesh=mesh, in_specs=in_specs, out_specs=out_specs, check_vma=False)
```
